256 devices in a mesh: ctx: 16 (over x, y), peer: 16 (over z, core).
Axes of the slice: x: 4, y: 4, z: 8, core: 2. Of those that a mesh axis runs over, the one named last changes fastest.
Arguments:
- queries: bfloat16 [16384, 4096], P(('ctx', 'peer')), may hold values from -120 to 120
- key_vectors: bfloat16 [16384, 4096], P(('ctx', 'peer')), may hold values from -6 to 6
- value_vectors: bfloat16 [16384, 4096], P(('ctx', 'peer')), may hold values from -6 to 6
- dispatch_plan: int32 [16], replicated, may hold values from 0 to 15, each once
Outputs:
- attended: bfloat16 [16384, 4096], P(('ctx', 'peer'))
The draws below stay inside these ranges and needn't reach their ends.
Inputs may be any that keep to these rules, and one draw needn't show every extreme that they name: `dispatch_plan`: a permutation: every value 0 to 15 once.
All inputs are finite; a program needn't handle non-finite values.
Results may differ from the reference program's by a relative error of at most 0.017.
Values may be sent and summed in bfloat16 or wider, within the bound.
No kernel may reach another device: no remote copies, remote signals or barrier semaphores. Data moves between devices by JAX's collectives and lax.ppermute only.
A program may use at most 128 MiB of HBM per device.

```python
import jax
import jax.numpy as jnp
from jax import lax

HEADS = 32
HEAD_DIM = 128
SPAN = 1024
NCH = 16
SEQ = 16384
HD = 4096


def shared_keys(key):
    return jnp.clip(jax.random.normal(key, (SEQ, HD), jnp.float32), -6.0, 6.0)


def draw_key_vectors(key, part):
    shared = shared_keys(key)
    return shared.astype(jnp.bfloat16)


def draw_queries(key, part):
    key = jax.random.fold_in(key, 7)
    own_rows = jnp.clip(jax.random.normal(key, (SEQ, HD), jnp.float32), -6.0, 6.0)
    return own_rows.astype(jnp.bfloat16)


def block_levels(rng, extent, cuts, smallest, largest):
    factor_of = 1.0
    for axis_at, shards_of in cuts:
        steps = jax.random.uniform(jax.random.fold_in(jax.random.fold_in(rng, 6), axis_at), (shards_of,), jnp.float32, smallest / len(cuts), largest / len(cuts))
        factor_of = factor_of * jnp.repeat(jnp.exp(steps), extent[axis_at] // shards_of).reshape((-1,) + (1,) * (len(extent) - 1 - axis_at))
    return factor_of


def noise(own_key, dims, spread, reach, split=(), kind=jnp.bfloat16):
    loudness = block_levels(own_key, dims, split, -0.22, 0.18) if split else 1.0
    array = jax.random.normal(own_key, dims, jnp.float32) * spread * loudness
    return jnp.minimum(jnp.maximum(array, -reach), reach).astype(kind)


def setup_inputs(seed: int = 0) -> dict:
    arg_keys = jax.random.split(jax.random.key(seed), 5)
    queries = draw_queries(jax.random.fold_in(arg_keys[4], 71), 0)
    key_vectors = draw_key_vectors(jax.random.fold_in(arg_keys[4], 71), 0)
    value_vectors = noise(arg_keys[2], (SEQ, HD), 1.0, 6.0, ((0, 256),))
    dispatch_plan = jax.random.permutation(arg_keys[3], NCH).astype(jnp.int32)
    return dict(queries=queries, key_vectors=key_vectors, value_vectors=value_vectors, dispatch_plan=dispatch_plan)


def reference(queries, key_vectors, value_vectors, dispatch_plan):
    span_ids = jnp.arange(SEQ, dtype=jnp.int32) // SPAN
    position = dispatch_plan[span_ids].astype(jnp.int32)
    score_scale = HEAD_DIM ** -0.5

    def heads_first(matrix):
        return matrix.reshape(SEQ, HEADS, HEAD_DIM).transpose(1, 0, 2)

    def one_head(inputs):
        q_head, k_head, v_head = inputs

        def one_block(block_inputs):
            q_block, q_place = block_inputs
            scores = jnp.dot(q_block, k_head.T, preferred_element_type=jnp.float32) * score_scale
            visible = position[None, :] <= q_place[:, None]
            top_score = jnp.max(jnp.where(visible, scores, -1e30), axis=1, keepdims=True)
            weights = jnp.where(visible, jnp.exp(scores - top_score), 0.0)
            totals = jnp.sum(weights, axis=1, keepdims=True)
            summed = jnp.dot(weights.astype(jnp.bfloat16), v_head, preferred_element_type=jnp.float32)
            return (summed / totals).astype(jnp.bfloat16)

        return lax.map(one_block, (q_head.reshape(SEQ // SPAN, SPAN, HEAD_DIM), position.reshape(SEQ // SPAN, SPAN)))

    outputs = lax.map(one_head, (heads_first(queries), heads_first(key_vectors), heads_first(value_vectors)))
    return outputs.reshape(HEADS, SEQ, HEAD_DIM).transpose(1, 0, 2).reshape(SEQ, HEADS * HEAD_DIM)
```

```python
import functools

import jax
import jax.numpy as jnp
from jax import lax
from jax.experimental import pallas as pl
from jax.experimental.pallas import tpu as pltpu
from jax.sharding import Mesh, PartitionSpec as P

HEAD_DIM = 128
PLACES = 16
ROWS = 64
QUERY_PLACES = 2
LOWEST = -1e30
TO_LOG2 = HEAD_DIM ** (-0.5) * 1.4426950408889634

GROUP = ("core", "x", "y")
RING = 8


def attend_kernel(halves, first, last, *refs):
    span_ref, q_ref = refs[0], refs[1]
    count = 1 + max(operand for block in halves for operand, _ in block)
    k_refs, v_refs = refs[2 : 2 + count], refs[2 + count : 2 + 2 * count]
    rest = refs[2 + 2 * count :]
    if not first:
        top_in, accum_in = rest[0], rest[1]
        rest = rest[2:]
    if last:
        (out_ref,) = rest
    else:
        top_out, accum_out = rest
    tile = QUERY_PLACES * 2 * ROWS

    def rows_of(pieces, places):
        return jnp.concatenate(
            [ref[index, span_ref[place]] for place in places for ref, index in pieces], axis=0
        )

    for step in range(PLACES // QUERY_PLACES):
        places = range(step * QUERY_PLACES, (step + 1) * QUERY_PLACES)
        seen = (step + 1) * QUERY_PLACES
        spot = pl.ds(step * tile, tile)
        q = rows_of([(q_ref, 0), (q_ref, 1)], places)
        if first:
            top = jnp.full((tile, 1), LOWEST, jnp.float32)
            accum = jnp.zeros((tile, 2 * HEAD_DIM), jnp.float32)
        else:
            top = top_in[spot, 0:1]
            accum = accum_in[spot]
        for block in halves:
            keys = rows_of([(k_refs[o], i) for o, i in block], range(seen))
            values = rows_of([(v_refs[o], i) for o, i in block], range(seen))
            scores = (
                lax.dot_general(
                    q, keys, (((1,), (1,)), ((), ())), preferred_element_type=jnp.float32
                )
                * TO_LOG2
            )
            row_place = lax.broadcasted_iota(jnp.int32, scores.shape, 0) // (2 * ROWS)
            key_place = lax.broadcasted_iota(jnp.int32, scores.shape, 1) // (2 * ROWS)
            scores = jnp.where(
                key_place <= row_place + step * QUERY_PLACES, scores, LOWEST
            )
            fresh = jnp.maximum(top, jnp.max(scores, axis=1, keepdims=True))
            weights = jnp.exp2(scores - fresh).astype(jnp.bfloat16)
            wide = jnp.concatenate([values, jnp.ones_like(values)], axis=1)
            accum = accum * jnp.exp2(top - fresh) + jnp.dot(
                weights, wide, preferred_element_type=jnp.float32
            )
            top = fresh
        if last:
            result = (accum[:, :HEAD_DIM] / accum[:, HEAD_DIM:]).astype(jnp.bfloat16)
            at = 0
            for place in places:
                for half in range(2):
                    out_ref[half, span_ref[place]] = result[at : at + ROWS]
                    at += ROWS
        else:
            top_out[spot] = jnp.broadcast_to(top, (tile, HEAD_DIM))
            accum_out[spot] = accum


def attend(span_of, q, keys, values, halves, state, last):
    first = state is None
    rows = PLACES * 2 * ROWS
    whole = pl.BlockSpec(memory_space=pltpu.VMEM)
    inputs = [q, *keys, *values] + ([] if first else list(state))
    if last:
        out_shape = jax.ShapeDtypeStruct(q.shape, jnp.bfloat16)
        out_specs = whole
    else:
        out_shape = (
            jax.ShapeDtypeStruct((rows, HEAD_DIM), jnp.float32),
            jax.ShapeDtypeStruct((rows, 2 * HEAD_DIM), jnp.float32),
        )
        out_specs = (whole, whole)
    pairs = PLACES * (PLACES + 1) // 2 * (2 * ROWS) ** 2 * len(halves)
    return pl.pallas_call(
        functools.partial(attend_kernel, halves, first, last),
        out_shape=out_shape,
        in_specs=[pl.BlockSpec(memory_space=pltpu.SMEM)] + [whole] * len(inputs),
        out_specs=out_specs,
        compiler_params=pltpu.CompilerParams(vmem_limit_bytes=40 * 2**20),
        cost_estimate=pl.CostEstimate(
            flops=8 * pairs * HEAD_DIM, bytes_accessed=8 * 2**20, transcendentals=pairs
        ),
    )(span_of, *inputs)


def local(queries, key_vectors, value_vectors, dispatch_plan):
    def to_heads(rows):
        return lax.all_to_all(rows, GROUP, split_axis=1, concat_axis=0, tiled=True).reshape(
            2, PLACES, ROWS, HEAD_DIM
        )

    up = [(i, (i + 1) % RING) for i in range(RING)]
    down = [(i, (i - 1) % RING) for i in range(RING)]
    span_of = jnp.argsort(dispatch_plan).astype(jnp.int32)

    def ring(own):
        ups, downs = [own], [own]
        for _ in range(3):
            ups.append(lax.ppermute(ups[-1], "z", up))
            downs.append(lax.ppermute(downs[-1], "z", down))
        far = (
            lax.ppermute(ups[-1][:1], "z", up),
            lax.ppermute(downs[-1][1:], "z", down),
        )
        return ups, downs, far

    k_own = to_heads(key_vectors)
    k_own, value_vectors = lax.optimization_barrier((k_own, value_vectors))
    v_own = to_heads(value_vectors)
    v_own, queries = lax.optimization_barrier((v_own, queries))
    q = to_heads(queries)
    k_up, k_down, k_far = ring(k_own)
    v_up, v_down, v_far = ring(v_own)

    def block(operand):
        return ((operand, 0), (operand, 1))

    state = attend(span_of, q, [k_own], [v_own], [block(0)], None, False)
    for step in (1, 2, 3):
        state = attend(
            span_of, q, [k_up[step]], [v_up[step]], [block(0)], state, False
        )
        state = attend(
            span_of, q, [k_down[step]], [v_down[step]], [block(0)], state, False
        )
    attended = attend(span_of, q, k_far, v_far, [((0, 0), (1, 0))], state, True)
    return lax.all_to_all(
        attended.reshape(2 * PLACES * ROWS, HEAD_DIM), GROUP, split_axis=0, concat_axis=1, tiled=True
    )


def solution(mesh):
    fine = Mesh(mesh.devices.reshape(4, 4, RING, 2), ("x", "y", "z", "core"))
    split = P(("x", "y", "z", "core"), None)
    return jax.shard_map(
        local, mesh=fine, in_specs=(split, split, split, P()), out_specs=split, check_vma=False
    )
```

```python
import functools

import jax
import jax.numpy as jnp
from jax import lax
from jax.experimental import pallas as pl
from jax.experimental.pallas import tpu as pltpu
from jax.sharding import Mesh, PartitionSpec as P

HEAD_DIM = 128
PLACES = 16
ROWS = 64
BLOCK = 2 * ROWS
TOKENS = PLACES * BLOCK
ONES = 16
QUERY_PLACES = 2
KEY_PLACES = 8
LOWEST = -1e30
TO_LOG2 = HEAD_DIM ** (-0.5) * 1.4426950408889634

GROUP = ("core", "x", "y")
RING = 8


def attend_kernel(first, last, *refs):
    span_ref, q_ref, low_ref, high_ref = refs[:4]
    rest = refs[4:]
    if not first:
        top_in, accum_in = rest[:2]
        rest = rest[2:]
    if last:
        out_ref = rest[0]
        rest = rest[1:]
    else:
        top_out, accum_out = rest[:2]
        rest = rest[2:]
    qt_ref, k_ref, vt_ref = rest
    tile = QUERY_PLACES * BLOCK

    for place in range(PLACES):
        at = slice(place * BLOCK, (place + 1) * BLOCK)
        span = span_ref[place]
        qt_ref[:, at] = jnp.concatenate([q_ref[0, span], q_ref[1, span]], axis=0).T
        k_ref[at, :] = jnp.concatenate([low_ref[span, 0], high_ref[span, 0]], axis=0)
        vt_ref[:HEAD_DIM, at] = jnp.concatenate([low_ref[span, 1], high_ref[span, 1]], axis=0).T
    vt_ref[HEAD_DIM:, :] = jnp.ones((ONES, TOKENS), jnp.bfloat16)

    items = []
    for step in range(PLACES // QUERY_PLACES):
        begin = step * QUERY_PLACES
        cuts = list(range(0, begin, KEY_PLACES)) + [begin, begin + QUERY_PLACES]
        pieces = list(zip(cuts[:-1], cuts[1:]))
        for number, (low, high) in enumerate(pieces):
            items.append((step, low, high, number == 0, number == len(pieces) - 1))
    key_place = lax.broadcasted_iota(jnp.int32, (tile, tile), 0) // BLOCK
    query_place = lax.broadcasted_iota(jnp.int32, (tile, tile), 1) // BLOCK
    hidden = key_place > query_place

    def scores_of(item):
        step, low, high, _, diagonal = item
        scores = TO_LOG2 * jnp.dot(
            k_ref[low * BLOCK : high * BLOCK, :],
            qt_ref[:, step * tile : (step + 1) * tile],
            preferred_element_type=jnp.float32,
        )
        return jnp.where(hidden, LOWEST, scores) if diagonal else scores

    ahead = scores_of(items[0])
    for number, (step, low, high, starts, ends) in enumerate(items):
        scores = ahead
        if number + 1 < len(items):
            ahead = scores_of(items[number + 1])
        spot = slice(step * tile, (step + 1) * tile)
        if starts:
            if first:
                top = jnp.full((1, tile), LOWEST, jnp.float32)
                accum = jnp.zeros((HEAD_DIM + ONES, tile), jnp.float32)
            else:
                top = top_in[0:1, spot]
                accum = accum_in[:, spot]
        fresh = jnp.maximum(top, jnp.max(scores, axis=0, keepdims=True))
        weights = jnp.exp2(scores - fresh).astype(jnp.bfloat16)
        accum = accum * jnp.exp2(top - fresh) + jnp.dot(
            vt_ref[:, low * BLOCK : high * BLOCK], weights, preferred_element_type=jnp.float32
        )
        top = fresh
        if not ends:
            continue
        if last:
            result = accum[:HEAD_DIM] / accum[HEAD_DIM : HEAD_DIM + 1]
            for inner in range(QUERY_PLACES):
                span = span_ref[step * QUERY_PLACES + inner]
                rows = result[:, inner * BLOCK : (inner + 1) * BLOCK].T.astype(jnp.bfloat16)
                out_ref[0, span] = rows[:ROWS]
                out_ref[1, span] = rows[ROWS:]
        else:
            top_out[:, spot] = jnp.broadcast_to(top, (8, tile))
            accum_out[:, spot] = accum


def attend(span_of, q, block, state, last):
    first = state is None
    whole = pl.BlockSpec(memory_space=pltpu.VMEM)
    inputs = [q, *block] + ([] if first else list(state))
    if last:
        out_shape = jax.ShapeDtypeStruct(q.shape, jnp.bfloat16)
        out_specs = whole
    else:
        out_shape = (
            jax.ShapeDtypeStruct((8, TOKENS), jnp.float32),
            jax.ShapeDtypeStruct((HEAD_DIM + ONES, TOKENS), jnp.float32),
        )
        out_specs = (whole, whole)
    pairs = PLACES * (PLACES + 1) // 2 * BLOCK**2
    return pl.pallas_call(
        functools.partial(attend_kernel, first, last),
        out_shape=out_shape,
        in_specs=[pl.BlockSpec(memory_space=pltpu.SMEM)] + [whole] * len(inputs),
        out_specs=out_specs,
        scratch_shapes=[
            pltpu.VMEM((HEAD_DIM, TOKENS), jnp.bfloat16),
            pltpu.VMEM((TOKENS, HEAD_DIM), jnp.bfloat16),
            pltpu.VMEM((HEAD_DIM + ONES, TOKENS), jnp.bfloat16),
        ],
        compiler_params=pltpu.CompilerParams(vmem_limit_bytes=32 * 2**20),
        cost_estimate=pl.CostEstimate(
            flops=8 * pairs * HEAD_DIM, bytes_accessed=4 * 2**20, transcendentals=pairs
        ),
    )(span_of, *inputs)


def local(queries, key_vectors, value_vectors, dispatch_plan):
    up = [(i, (i + 1) % RING) for i in range(RING)]
    down = [(i, (i - 1) % RING) for i in range(RING)]
    places = jnp.arange(PLACES, dtype=jnp.int32)
    span_of = jnp.sum(
        jnp.where(dispatch_plan[None, :] == places[:, None], places[None, :], 0), axis=1
    )

    def by_head(rows):
        return rows.reshape(ROWS, 2 * PLACES, HEAD_DIM).transpose(1, 0, 2)

    pairs = jnp.stack([by_head(key_vectors), by_head(value_vectors)], axis=1)
    pairs = lax.all_to_all(pairs, GROUP, split_axis=0, concat_axis=0, tiled=True)
    pairs, queries = lax.optimization_barrier((pairs, queries))
    halves = pairs.reshape(2, PLACES, 2, ROWS, HEAD_DIM)
    ups = [(halves[0], halves[1])]
    downs = [(halves[0], halves[1])]
    for _ in range(3):
        ups.append(tuple(lax.ppermute(half, "z", up) for half in ups[-1]))
        downs.append(tuple(lax.ppermute(half, "z", down) for half in downs[-1]))
    far = (lax.ppermute(ups[-1][0], "z", up), lax.ppermute(downs[-1][1], "z", down))

    q = lax.all_to_all(queries, GROUP, split_axis=1, concat_axis=0, tiled=True)
    q = q.reshape(2, PLACES, ROWS, HEAD_DIM)

    state = attend(span_of, q, ups[0], None, False)
    for step in (1, 2, 3):
        state = attend(span_of, q, ups[step], state, False)
        state = attend(span_of, q, downs[step], state, False)
    attended = attend(span_of, q, far, state, True)
    return lax.all_to_all(
        attended.reshape(TOKENS, HEAD_DIM), GROUP, split_axis=0, concat_axis=1, tiled=True
    )


def solution(mesh):
    fine = Mesh(mesh.devices.reshape(4, 4, RING, 2), ("x", "y", "z", "core"))
    split = P(("x", "y", "z", "core"), None)
    return jax.shard_map(
        local, mesh=fine, in_specs=(split, split, split, P()), out_specs=split, check_vma=False
    )
```

```python
import functools

import jax
import jax.numpy as jnp
from jax import lax
from jax.experimental import pallas as pl
from jax.experimental.pallas import tpu as pltpu
from jax.sharding import Mesh, PartitionSpec as P

HEAD_DIM = 128
PLACES = 16
ROWS = 64
BLOCK = 2 * ROWS
TOKENS = PLACES * BLOCK
ONES = 16
QUERY_PLACES = 2
KEY_PLACES = 8
LOWEST = -1e30
MARGIN = 30.0
TO_LOG2 = HEAD_DIM ** (-0.5) * 1.4426950408889634

GROUP = ("core", "x", "y")
RING = 8


def attend_kernel(first, last, *refs):
    span_ref, q_ref, low_ref, high_ref = refs[:4]
    rest = refs[4:]
    if not first:
        top_in, accum_in = rest[:2]
        rest = rest[2:]
    if last:
        out_ref = rest[0]
        rest = rest[1:]
    else:
        top_out, accum_out = rest[:2]
        rest = rest[2:]
    qt_ref, k_ref, vt_ref = rest
    tile = QUERY_PLACES * BLOCK

    for place in range(PLACES):
        at = slice(place * BLOCK, (place + 1) * BLOCK)
        span = span_ref[place]
        scaled = TO_LOG2 * jnp.concatenate([q_ref[0, span], q_ref[1, span]], axis=0).astype(
            jnp.float32
        )
        coarse = scaled.astype(jnp.bfloat16)
        qt_ref[:HEAD_DIM, at] = coarse.T
        qt_ref[HEAD_DIM:, at] = (scaled - coarse.astype(jnp.float32)).astype(jnp.bfloat16).T
        keys = jnp.concatenate([low_ref[span, 0], high_ref[span, 0]], axis=0)
        k_ref[at, :HEAD_DIM] = keys
        k_ref[at, HEAD_DIM:] = keys
        vt_ref[:HEAD_DIM, at] = jnp.concatenate([low_ref[span, 1], high_ref[span, 1]], axis=0).T
    vt_ref[HEAD_DIM:, :] = jnp.ones((ONES, TOKENS), jnp.bfloat16)

    items = []
    for step in range(PLACES // QUERY_PLACES):
        begin = step * QUERY_PLACES
        cuts = list(range(0, begin, KEY_PLACES)) + [begin, begin + QUERY_PLACES]
        pieces = list(zip(cuts[:-1], cuts[1:]))
        for number, (low, high) in enumerate(pieces):
            items.append((step, low, high, number == 0, number == len(pieces) - 1))
    key_place = lax.broadcasted_iota(jnp.int32, (tile, tile), 0) // BLOCK
    query_place = lax.broadcasted_iota(jnp.int32, (tile, tile), 1) // BLOCK
    hidden = key_place > query_place

    def scores_of(item):
        step, low, high, _, diagonal = item
        scores = jnp.dot(
            k_ref[low * BLOCK : high * BLOCK, :],
            qt_ref[:, step * tile : (step + 1) * tile],
            preferred_element_type=jnp.float32,
        )
        return jnp.where(hidden, LOWEST, scores) if diagonal else scores

    def sweep(steady):
        excess = jnp.full((1, tile), LOWEST, jnp.float32)
        ahead = scores_of(items[0])
        for number, (step, low, high, starts, ends) in enumerate(items):
            scores = ahead
            if number + 1 < len(items):
                ahead = scores_of(items[number + 1])
            spot = slice(step * tile, (step + 1) * tile)
            if starts:
                if first:
                    top = jnp.full((1, tile), LOWEST, jnp.float32)
                    accum = jnp.zeros((HEAD_DIM + ONES, tile), jnp.float32)
                else:
                    top = top_in[0:1, spot]
                    accum = accum_in[:, spot]
            peak = jnp.max(scores, axis=0, keepdims=True)
            if steady:
                excess = jnp.maximum(excess, peak - top)
            else:
                fresh = jnp.maximum(top, peak)
                accum = accum * jnp.exp2(top - fresh)
                top = fresh
            weights = jnp.exp2(scores - top).astype(jnp.bfloat16)
            accum = accum + jnp.dot(
                vt_ref[:, low * BLOCK : high * BLOCK], weights, preferred_element_type=jnp.float32
            )
            if not ends:
                continue
            if last:
                result = accum[:HEAD_DIM] / accum[HEAD_DIM : HEAD_DIM + 1]
                for inner in range(QUERY_PLACES):
                    span = span_ref[step * QUERY_PLACES + inner]
                    rows = result[:, inner * BLOCK : (inner + 1) * BLOCK].T.astype(jnp.bfloat16)
                    out_ref[0, span] = rows[:ROWS]
                    out_ref[1, span] = rows[ROWS:]
            else:
                top_out[:, spot] = jnp.broadcast_to(top, (8, tile))
                accum_out[:, spot] = accum
        return jnp.max(excess)

    if first:
        sweep(False)
    else:
        passed = sweep(True) > MARGIN

        @pl.when(passed)
        def _():
            sweep(False)


def attend(span_of, q, block, state, last):
    first = state is None
    whole = pl.BlockSpec(memory_space=pltpu.VMEM)
    inputs = [q, *block] + ([] if first else list(state))
    if last:
        out_shape = jax.ShapeDtypeStruct(q.shape, jnp.bfloat16)
        out_specs = whole
    else:
        out_shape = (
            jax.ShapeDtypeStruct((8, TOKENS), jnp.float32),
            jax.ShapeDtypeStruct((HEAD_DIM + ONES, TOKENS), jnp.float32),
        )
        out_specs = (whole, whole)
    pairs = PLACES * (PLACES + 1) // 2 * BLOCK**2
    return pl.pallas_call(
        functools.partial(attend_kernel, first, last),
        out_shape=out_shape,
        in_specs=[pl.BlockSpec(memory_space=pltpu.SMEM)] + [whole] * len(inputs),
        out_specs=out_specs,
        scratch_shapes=[
            pltpu.VMEM((2 * HEAD_DIM, TOKENS), jnp.bfloat16),
            pltpu.VMEM((TOKENS, 2 * HEAD_DIM), jnp.bfloat16),
            pltpu.VMEM((HEAD_DIM + ONES, TOKENS), jnp.bfloat16),
        ],
        compiler_params=pltpu.CompilerParams(vmem_limit_bytes=32 * 2**20),
        cost_estimate=pl.CostEstimate(
            flops=8 * pairs * HEAD_DIM, bytes_accessed=4 * 2**20, transcendentals=pairs
        ),
    )(span_of, *inputs)


def local(queries, key_vectors, value_vectors, dispatch_plan):
    up = [(i, (i + 1) % RING) for i in range(RING)]
    down = [(i, (i - 1) % RING) for i in range(RING)]
    places = jnp.arange(PLACES, dtype=jnp.int32)
    span_of = jnp.sum(
        jnp.where(dispatch_plan[None, :] == places[:, None], places[None, :], 0), axis=1
    )

    def by_head(rows):
        return rows.reshape(ROWS, 2 * PLACES, HEAD_DIM).transpose(1, 0, 2)

    pairs = jnp.stack([by_head(key_vectors), by_head(value_vectors)], axis=1)
    pairs = lax.all_to_all(pairs, GROUP, split_axis=0, concat_axis=0, tiled=True)
    pairs, queries = lax.optimization_barrier((pairs, queries))
    halves = pairs.reshape(2, PLACES, 2, ROWS, HEAD_DIM)
    ups = [(halves[0], halves[1])]
    downs = [(halves[0], halves[1])]
    for _ in range(3):
        ups.append(tuple(lax.ppermute(half, "z", up) for half in ups[-1]))
        downs.append(tuple(lax.ppermute(half, "z", down) for half in downs[-1]))
    far = (lax.ppermute(ups[-1][0], "z", up), lax.ppermute(downs[-1][1], "z", down))

    q = lax.all_to_all(queries, GROUP, split_axis=1, concat_axis=0, tiled=True)
    q = q.reshape(2, PLACES, ROWS, HEAD_DIM)

    state = attend(span_of, q, ups[0], None, False)
    for step in (1, 2, 3):
        state = attend(span_of, q, ups[step], state, False)
        state = attend(span_of, q, downs[step], state, False)
    attended = attend(span_of, q, far, state, True)
    return lax.all_to_all(
        attended.reshape(TOKENS, HEAD_DIM), GROUP, split_axis=0, concat_axis=1, tiled=True
    )


def solution(mesh):
    fine = Mesh(mesh.devices.reshape(4, 4, RING, 2), ("x", "y", "z", "core"))
    split = P(("x", "y", "z", "core"), None)
    return jax.shard_map(
        local, mesh=fine, in_specs=(split, split, split, P()), out_specs=split, check_vma=False
    )
```

```python
import functools

import jax
import jax.numpy as jnp
from jax import lax
from jax.experimental import pallas as pl
from jax.experimental.pallas import tpu as pltpu
from jax.sharding import Mesh, PartitionSpec as P

HEAD_DIM = 128
PLACES = 16
ROWS = 64
BLOCK = 2 * ROWS
TOKENS = PLACES * BLOCK
ONES = 16
QUERY_PLACES = 2
KEY_PLACES = 8
LOWEST = -1e30
MARGIN = 30.0
TO_LOG2 = HEAD_DIM ** (-0.5) * 1.4426950408889634

GROUP = ("core", "x", "y")
RING = 8


def attend_kernel(first, last, *refs):
    span_ref, q_ref, low_ref, high_ref = refs[:4]
    rest = refs[4:]
    if not first:
        top_in, accum_in = rest[:2]
        rest = rest[2:]
    if last:
        out_ref = rest[0]
        rest = rest[1:]
    else:
        top_out, accum_out = rest[:2]
        rest = rest[2:]
    if first:
        qt_ref, k_ref, vt_ref = rest
    else:
        qt_ref = q_ref
        k_ref, vt_ref = rest
    tile = QUERY_PLACES * BLOCK

    for place in range(PLACES):
        at = slice(place * BLOCK, (place + 1) * BLOCK)
        span = span_ref[place]
        if first:
            scaled = TO_LOG2 * jnp.concatenate([q_ref[0, span], q_ref[1, span]], axis=0).astype(
                jnp.float32
            )
            coarse = scaled.astype(jnp.bfloat16)
            qt_ref[:HEAD_DIM, at] = coarse.T
            qt_ref[HEAD_DIM:, at] = (scaled - coarse.astype(jnp.float32)).astype(jnp.bfloat16).T
        keys = jnp.concatenate([low_ref[span, 0], high_ref[span, 0]], axis=0)
        k_ref[at, :HEAD_DIM] = keys
        k_ref[at, HEAD_DIM:] = keys
        vt_ref[:HEAD_DIM, at] = jnp.concatenate([low_ref[span, 1], high_ref[span, 1]], axis=0).T
    vt_ref[HEAD_DIM:, :] = jnp.ones((ONES, TOKENS), jnp.bfloat16)

    items = []
    for step in range(PLACES // QUERY_PLACES):
        begin = step * QUERY_PLACES
        cuts = list(range(0, begin, KEY_PLACES)) + [begin, begin + QUERY_PLACES]
        pieces = list(zip(cuts[:-1], cuts[1:]))
        for number, (low, high) in enumerate(pieces):
            items.append((step, low, high, number == 0, number == len(pieces) - 1))
    key_place = lax.broadcasted_iota(jnp.int32, (tile, tile), 0) // BLOCK
    query_place = lax.broadcasted_iota(jnp.int32, (tile, tile), 1) // BLOCK
    hidden = key_place > query_place

    def scores_of(item):
        step, low, high, _, diagonal = item
        scores = jnp.dot(
            k_ref[low * BLOCK : high * BLOCK, :],
            qt_ref[:, step * tile : (step + 1) * tile],
            preferred_element_type=jnp.float32,
        )
        return jnp.where(hidden, LOWEST, scores) if diagonal else scores

    def sweep(steady):
        excess = jnp.full((1, tile), LOWEST, jnp.float32)
        ahead = scores_of(items[0])
        for number, (step, low, high, starts, ends) in enumerate(items):
            scores = ahead
            if number + 1 < len(items):
                ahead = scores_of(items[number + 1])
            spot = slice(step * tile, (step + 1) * tile)
            if starts:
                if first:
                    top = jnp.full((1, tile), LOWEST, jnp.float32)
                    accum = jnp.zeros((HEAD_DIM + ONES, tile), jnp.float32)
                else:
                    top = top_in[0:1, spot]
                    accum = accum_in[:, spot]
            peak = jnp.max(scores, axis=0, keepdims=True)
            if steady:
                excess = jnp.maximum(excess, peak - top)
            else:
                fresh = jnp.maximum(top, peak)
                accum = accum * jnp.exp2(top - fresh)
                top = fresh
            weights = jnp.exp2(scores - top).astype(jnp.bfloat16)
            accum = accum + jnp.dot(
                vt_ref[:, low * BLOCK : high * BLOCK], weights, preferred_element_type=jnp.float32
            )
            if not ends:
                continue
            if last:
                result = accum[:HEAD_DIM] / accum[HEAD_DIM : HEAD_DIM + 1]
                for inner in range(QUERY_PLACES):
                    span = span_ref[step * QUERY_PLACES + inner]
                    rows = result[:, inner * BLOCK : (inner + 1) * BLOCK].T.astype(jnp.bfloat16)
                    out_ref[0, span] = rows[:ROWS]
                    out_ref[1, span] = rows[ROWS:]
            else:
                top_out[:, spot] = jnp.broadcast_to(top, (8, tile))
                accum_out[:, spot] = accum
        return jnp.max(excess)

    if first:
        sweep(False)
    else:
        passed = sweep(True) > MARGIN

        @pl.when(passed)
        def _():
            sweep(False)


def attend(span_of, q, block, state, last):
    first = state is None
    whole = pl.BlockSpec(memory_space=pltpu.VMEM)
    inputs = [q, *block] + ([] if first else list(state))
    if last:
        out_shape = jax.ShapeDtypeStruct((2, PLACES, ROWS, HEAD_DIM), jnp.bfloat16)
        out_specs = whole
    else:
        out_shape = (
            jax.ShapeDtypeStruct((8, TOKENS), jnp.float32),
            jax.ShapeDtypeStruct((HEAD_DIM + ONES, TOKENS), jnp.float32),
        )
        out_specs = (whole, whole)
        if first:
            out_shape += (jax.ShapeDtypeStruct((2 * HEAD_DIM, TOKENS), jnp.bfloat16),)
            out_specs += (whole,)
    pairs = PLACES * (PLACES + 1) // 2 * BLOCK**2
    return pl.pallas_call(
        functools.partial(attend_kernel, first, last),
        out_shape=out_shape,
        in_specs=[pl.BlockSpec(memory_space=pltpu.SMEM)] + [whole] * len(inputs),
        out_specs=out_specs,
        scratch_shapes=[
            pltpu.VMEM((TOKENS, 2 * HEAD_DIM), jnp.bfloat16),
            pltpu.VMEM((HEAD_DIM + ONES, TOKENS), jnp.bfloat16),
        ],
        compiler_params=pltpu.CompilerParams(vmem_limit_bytes=32 * 2**20),
        cost_estimate=pl.CostEstimate(
            flops=8 * pairs * HEAD_DIM, bytes_accessed=4 * 2**20, transcendentals=pairs
        ),
    )(span_of, *inputs)


def local(queries, key_vectors, value_vectors, dispatch_plan):
    up = [(i, (i + 1) % RING) for i in range(RING)]
    down = [(i, (i - 1) % RING) for i in range(RING)]
    places = jnp.arange(PLACES, dtype=jnp.int32)
    span_of = jnp.sum(
        jnp.where(dispatch_plan[None, :] == places[:, None], places[None, :], 0), axis=1
    )

    def by_head(rows):
        return rows.reshape(ROWS, 2 * PLACES, HEAD_DIM).transpose(1, 0, 2)

    pairs = jnp.stack([by_head(key_vectors), by_head(value_vectors)], axis=1)
    pairs = lax.all_to_all(pairs, GROUP, split_axis=0, concat_axis=0, tiled=True)
    pairs, queries = lax.optimization_barrier((pairs, queries))
    halves = pairs.reshape(2, PLACES, 2, ROWS, HEAD_DIM)
    ups = [(halves[0], halves[1])]
    downs = [(halves[0], halves[1])]
    for _ in range(3):
        ups.append(tuple(lax.ppermute(half, "z", up) for half in ups[-1]))
        downs.append(tuple(lax.ppermute(half, "z", down) for half in downs[-1]))
    far = (lax.ppermute(ups[-1][0], "z", up), lax.ppermute(downs[-1][1], "z", down))

    q = lax.all_to_all(queries, GROUP, split_axis=1, concat_axis=0, tiled=True)
    q = q.reshape(2, PLACES, ROWS, HEAD_DIM)

    *state, q = attend(span_of, q, ups[0], None, False)
    for step in (1, 2, 3):
        state = attend(span_of, q, ups[step], state, False)
        state = attend(span_of, q, downs[step], state, False)
    attended = attend(span_of, q, far, state, True)
    return lax.all_to_all(
        attended.reshape(TOKENS, HEAD_DIM), GROUP, split_axis=0, concat_axis=1, tiled=True
    )


def solution(mesh):
    fine = Mesh(mesh.devices.reshape(4, 4, RING, 2), ("x", "y", "z", "core"))
    split = P(("x", "y", "z", "core"), None)
    return jax.shard_map(
        local, mesh=fine, in_specs=(split, split, split, P()), out_specs=split, check_vma=False
    )
```

```python
import functools

import jax
import jax.numpy as jnp
from jax import lax
from jax.experimental import pallas as pl
from jax.experimental.pallas import tpu as pltpu
from jax.sharding import Mesh, PartitionSpec as P

HEAD_DIM = 128
PLACES = 16
ROWS = 64
BLOCK = 2 * ROWS
TOKENS = PLACES * BLOCK
ONES = 16
QUERY_PLACES = 4
KEY_PLACES = 4
LOWEST = -1e30
MARGIN = 30.0
TO_LOG2 = HEAD_DIM ** (-0.5) * 1.4426950408889634

GROUP = ("core", "x", "y")
RING = 8


def attend_kernel(first, last, *refs):
    span_ref, q_ref, low_ref, high_ref = refs[:4]
    rest = refs[4:]
    if not first:
        top_in, accum_in = rest[:2]
        rest = rest[2:]
    if last:
        out_ref = rest[0]
        rest = rest[1:]
    else:
        top_out, accum_out = rest[:2]
        rest = rest[2:]
    if first:
        qt_ref, k_ref, vt_ref = rest
    else:
        qt_ref = q_ref
        k_ref, vt_ref = rest
    tile = QUERY_PLACES * BLOCK

    for place in range(PLACES):
        at = slice(place * BLOCK, (place + 1) * BLOCK)
        span = span_ref[place]
        if first:
            scaled = TO_LOG2 * jnp.concatenate([q_ref[0, span], q_ref[1, span]], axis=0).astype(
                jnp.float32
            )
            coarse = scaled.astype(jnp.bfloat16)
            qt_ref[:HEAD_DIM, at] = coarse.T
            qt_ref[HEAD_DIM:, at] = (scaled - coarse.astype(jnp.float32)).astype(jnp.bfloat16).T
        keys = jnp.concatenate([low_ref[span, 0], high_ref[span, 0]], axis=0)
        k_ref[at, :HEAD_DIM] = keys
        k_ref[at, HEAD_DIM:] = keys
        vt_ref[:HEAD_DIM, at] = jnp.concatenate([low_ref[span, 1], high_ref[span, 1]], axis=0).T
    vt_ref[HEAD_DIM:, :] = jnp.ones((ONES, TOKENS), jnp.bfloat16)

    items = []
    for step in range(PLACES // QUERY_PLACES):
        begin = step * QUERY_PLACES
        cuts = list(range(0, begin, KEY_PLACES)) + [begin, begin + QUERY_PLACES]
        pieces = list(zip(cuts[:-1], cuts[1:]))
        for number, (low, high) in enumerate(pieces):
            items.append((step, low, high, number == 0, number == len(pieces) - 1))
    key_place = lax.broadcasted_iota(jnp.int32, (tile, tile), 0) // BLOCK
    query_place = lax.broadcasted_iota(jnp.int32, (tile, tile), 1) // BLOCK
    hidden = key_place > query_place

    def scores_of(item):
        step, low, high, _, diagonal = item
        scores = jnp.dot(
            k_ref[low * BLOCK : high * BLOCK, :],
            qt_ref[:, step * tile : (step + 1) * tile],
            preferred_element_type=jnp.float32,
        )
        return jnp.where(hidden, LOWEST, scores) if diagonal else scores

    def sweep(steady):
        excess = jnp.full((1, tile), LOWEST, jnp.float32)
        ahead = scores_of(items[0])
        for number, (step, low, high, starts, ends) in enumerate(items):
            scores = ahead
            if number + 1 < len(items):
                ahead = scores_of(items[number + 1])
            spot = slice(step * tile, (step + 1) * tile)
            if starts:
                if first:
                    top = jnp.full((1, tile), LOWEST, jnp.float32)
                    accum = jnp.zeros((HEAD_DIM + ONES, tile), jnp.float32)
                else:
                    top = top_in[0:1, spot]
                    accum = accum_in[:, spot]
            peak = jnp.max(scores, axis=0, keepdims=True)
            if steady:
                excess = jnp.maximum(excess, peak - top)
            else:
                fresh = jnp.maximum(top, peak)
                accum = accum * jnp.exp2(top - fresh)
                top = fresh
            weights = jnp.exp2(scores - top).astype(jnp.bfloat16)
            accum = accum + jnp.dot(
                vt_ref[:, low * BLOCK : high * BLOCK], weights, preferred_element_type=jnp.float32
            )
            if not ends:
                continue
            if last:
                result = accum[:HEAD_DIM] / accum[HEAD_DIM : HEAD_DIM + 1]
                for inner in range(QUERY_PLACES):
                    span = span_ref[step * QUERY_PLACES + inner]
                    rows = result[:, inner * BLOCK : (inner + 1) * BLOCK].T.astype(jnp.bfloat16)
                    out_ref[0, span] = rows[:ROWS]
                    out_ref[1, span] = rows[ROWS:]
            else:
                top_out[:, spot] = jnp.broadcast_to(top, (8, tile))
                accum_out[:, spot] = accum
        return jnp.max(excess)

    if first:
        sweep(False)
    else:
        passed = sweep(True) > MARGIN

        @pl.when(passed)
        def _():
            sweep(False)


def attend(span_of, q, block, state, last):
    first = state is None
    whole = pl.BlockSpec(memory_space=pltpu.VMEM)
    inputs = [q, *block] + ([] if first else list(state))
    if last:
        out_shape = jax.ShapeDtypeStruct((2, PLACES, ROWS, HEAD_DIM), jnp.bfloat16)
        out_specs = whole
    else:
        out_shape = (
            jax.ShapeDtypeStruct((8, TOKENS), jnp.float32),
            jax.ShapeDtypeStruct((HEAD_DIM + ONES, TOKENS), jnp.float32),
        )
        out_specs = (whole, whole)
        if first:
            out_shape += (jax.ShapeDtypeStruct((2 * HEAD_DIM, TOKENS), jnp.bfloat16),)
            out_specs += (whole,)
    pairs = PLACES * (PLACES + 1) // 2 * BLOCK**2
    return pl.pallas_call(
        functools.partial(attend_kernel, first, last),
        out_shape=out_shape,
        in_specs=[pl.BlockSpec(memory_space=pltpu.SMEM)] + [whole] * len(inputs),
        out_specs=out_specs,
        scratch_shapes=[
            pltpu.VMEM((TOKENS, 2 * HEAD_DIM), jnp.bfloat16),
            pltpu.VMEM((HEAD_DIM + ONES, TOKENS), jnp.bfloat16),
        ],
        compiler_params=pltpu.CompilerParams(vmem_limit_bytes=32 * 2**20),
        cost_estimate=pl.CostEstimate(
            flops=8 * pairs * HEAD_DIM, bytes_accessed=4 * 2**20, transcendentals=pairs
        ),
    )(span_of, *inputs)


def local(queries, key_vectors, value_vectors, dispatch_plan):
    up = [(i, (i + 1) % RING) for i in range(RING)]
    down = [(i, (i - 1) % RING) for i in range(RING)]
    places = jnp.arange(PLACES, dtype=jnp.int32)
    span_of = jnp.sum(
        jnp.where(dispatch_plan[None, :] == places[:, None], places[None, :], 0), axis=1
    )

    def by_head(rows):
        return rows.reshape(ROWS, 2 * PLACES, HEAD_DIM).transpose(1, 0, 2)

    pairs = jnp.stack([by_head(key_vectors), by_head(value_vectors)], axis=1)
    pairs = lax.all_to_all(pairs, GROUP, split_axis=0, concat_axis=0, tiled=True)
    pairs, queries = lax.optimization_barrier((pairs, queries))
    halves = pairs.reshape(2, PLACES, 2, ROWS, HEAD_DIM)
    ups = [(halves[0], halves[1])]
    downs = [(halves[0], halves[1])]
    for _ in range(3):
        ups.append(tuple(lax.ppermute(half, "z", up) for half in ups[-1]))
        downs.append(tuple(lax.ppermute(half, "z", down) for half in downs[-1]))
    far = (lax.ppermute(ups[-1][0], "z", up), lax.ppermute(downs[-1][1], "z", down))

    q = lax.all_to_all(queries, GROUP, split_axis=1, concat_axis=0, tiled=True)
    q = q.reshape(2, PLACES, ROWS, HEAD_DIM)

    *state, q = attend(span_of, q, ups[0], None, False)
    for step in (1, 2, 3):
        state = attend(span_of, q, ups[step], state, False)
        state = attend(span_of, q, downs[step], state, False)
    attended = attend(span_of, q, far, state, True)
    return lax.all_to_all(
        attended.reshape(TOKENS, HEAD_DIM), GROUP, split_axis=0, concat_axis=1, tiled=True
    )


def solution(mesh):
    fine = Mesh(mesh.devices.reshape(4, 4, RING, 2), ("x", "y", "z", "core"))
    split = P(("x", "y", "z", "core"), None)
    return jax.shard_map(
        local, mesh=fine, in_specs=(split, split, split, P()), out_specs=split, check_vma=False
    )
```
